32 devices in a mesh: fine: 4 (over x, core), coarse: 8 (over z, y).
Axes of the slice: x: 2, y: 2, z: 4, core: 2. Of those that a mesh axis runs over, the one named last changes fastest.
Arguments:
- query_rows: bfloat16 [8192, 768], P(('coarse', 'fine')), may hold values from -6 to 6
- key_rows: bfloat16 [8192, 768], P(('coarse', 'fine')), may hold values from -6 to 6
- value_rows: bfloat16 [8192, 768], P(('coarse', 'fine')), may hold values from -6 to 6
- distance_slope: float32 [12], replicated, may hold values from 0.4 to 1.6
- out_weight: bfloat16 [768, 768], P('coarse'), may hold values from -0.21875 to 0.21875
Outputs:
- mixed: bfloat16 [8192, 768], P(('coarse', 'fine'))
The draws below stay inside these ranges and needn't reach their ends.
All inputs are finite; a program needn't handle non-finite values.
Results may differ from the reference program's by a relative error of at most 0.0065.
Values may be sent and summed in bfloat16 or wider, within the bound.
A program may use at most 64 MiB of HBM per device.

```python
import math
import jax
import jax.numpy as jnp
from jax import lax

HEADS = 12
D = 768
BLOCK = 128
TOKENS = 8192


def slow_part(key_phase):
    position = jnp.arange(TOKENS, dtype=jnp.int32)
    phases = jax.random.uniform(key_phase, (12, D), minval=-math.pi, maxval=math.pi)
    total = jnp.zeros((TOKENS, D), jnp.float32)
    for octave in range(1, 13):
        period_len = max(TOKENS // 2 ** octave, 2)
        amplitude = 0.8 if octave <= 6 else 0.35
        angle = (position % period_len).astype(jnp.float32) * (2.0 * math.pi / period_len)
        total = total + amplitude * jnp.sin(angle[:, None] + phases[octave - 1][None, :])
    return total


def paired_draw(key_base):
    seed_key = jax.random.fold_in(key_base, 17)
    key_query = jax.random.fold_in(seed_key, 0)
    key_keyed = jax.random.fold_in(seed_key, 1)
    key_qslow = jax.random.fold_in(seed_key, 4)
    key_kslow = jax.random.fold_in(seed_key, 5)
    shape_all = (TOKENS, D)
    query_slow = slow_part(key_qslow)
    key_slow = slow_part(key_kslow)
    query_draw = jnp.clip(0.8 * jax.random.normal(key_query, shape_all) + query_slow, -6.0, 6.0)
    key_draw = jnp.clip(0.8 * jax.random.normal(key_keyed, shape_all) + key_slow, -6.0, 6.0)
    return (query_draw, key_draw)


def draw_query_rows(key, part):
    return paired_draw(key)[0].astype(jnp.bfloat16)


def draw_key_rows(key, part):
    return paired_draw(key)[1].astype(jnp.bfloat16)


def draw_value_rows(key, part):
    seed_key = jax.random.fold_in(key, 29)
    key_rough, key_phase = jax.random.split(seed_key, 2)
    position = jnp.arange(TOKENS, dtype=jnp.float32)[:, None]
    phases = jax.random.uniform(key_phase, (8, D), minval=-math.pi, maxval=math.pi)
    smooth = jnp.zeros((TOKENS, D), jnp.float32)
    for octave in range(8):
        period_len = TOKENS / 2.0 ** octave
        smooth = smooth + 0.35 * jnp.sin(position * (2.0 * math.pi / period_len) + phases[octave][None, :])
    value_draw = 0.8 * jax.random.normal(key_rough, (TOKENS, D)) + smooth
    return jnp.clip(value_draw, -6.0, 6.0).astype(jnp.bfloat16)


def block_levels(own_key, extent, cuts, least, largest):
    loudness, own = 1.0, jax.random.fold_in(own_key, 6)
    for axis_at, shards_of in cuts:
        heights = jnp.exp(jax.random.uniform(jax.random.fold_in(own, axis_at), (shards_of,), jnp.float32, least / len(cuts), largest / len(cuts)))
        loudness = loudness * jnp.repeat(heights, extent[axis_at] // shards_of).reshape([-1 if axis == axis_at else 1 for axis in range(len(extent))])
    return loudness


def bell_draw(rng, shape, spread, reach, cuts=(), kind=jnp.bfloat16):
    gain = block_levels(rng, shape, cuts, -0.22, 0.18) if cuts else 1.0
    result = jax.random.normal(rng, shape, jnp.float32) * spread * gain
    return jnp.minimum(jnp.maximum(result, -reach), reach).astype(kind)


def setup_inputs(seed: int = 0) -> dict:
    key_list = jax.random.split(jax.random.key(seed), 6)
    query_rows = draw_query_rows(jax.random.fold_in(key_list[5], 71), 0)
    key_rows = draw_key_rows(jax.random.fold_in(key_list[5], 71), 0)
    value_rows = draw_value_rows(jax.random.fold_in(key_list[5], 71), 0)
    distance_slope = jnp.clip(jnp.exp(jax.random.uniform(key_list[3], (HEADS,), jnp.float32, math.log(0.4), math.log(1.6))), 0.4, 1.6)
    out_weight = bell_draw(key_list[4], (D, D), D ** -0.5, 0.21875, ((0, 8),))
    return dict(query_rows=query_rows, key_rows=key_rows, value_rows=value_rows, distance_slope=distance_slope, out_weight=out_weight)


LOG_TWO = math.log(2.0)

def coarsen(row_data):
    dims_all = row_data.shape
    paired = row_data.reshape(dims_all[:-2] + (dims_all[-2] // 2, 2, dims_all[-1])).astype(jnp.float32)
    return ((paired[..., 0, :] + paired[..., 1, :]) * 0.5).astype(jnp.bfloat16)

def attend(queries, key_group, value_group, level_gain):
    groups, query_count, width_all = queries.shape
    key_count = key_group.shape[1]
    head_count = level_gain.shape[0]
    head_size = width_all // head_count
    q_heads = queries.astype(jnp.float32).reshape(groups, query_count, head_count, head_size)
    k_heads = key_group.astype(jnp.float32).reshape(groups, key_count, head_count, head_size)
    v_heads = value_group.astype(jnp.float32).reshape(groups, key_count, head_count, head_size)
    scores = jnp.einsum('gqhe,gkhe->ghqk', q_heads, k_heads) * (1.0 / math.sqrt(head_size)) + level_gain[None, :, None, None]
    row_max = lax.optimization_barrier(jnp.max(scores, axis=3))
    p_weights = jnp.exp(scores - row_max[..., None]).astype(jnp.bfloat16)
    row_sum = lax.optimization_barrier(jnp.sum(p_weights.astype(jnp.float32), axis=3))
    weighted = jnp.einsum('ghqk,gkhe->gqhe', p_weights.astype(jnp.float32), v_heads)
    return (jnp.transpose(row_max, (0, 2, 1)).reshape(groups * query_count, head_count), weighted.reshape(groups * query_count, width_all), jnp.transpose(row_sum, (0, 2, 1)).reshape(groups * query_count, head_count))

def level_stats(q_now, k_now, v_now, level_now, distance_slope):
    row_count, width_all = q_now.shape
    level_gain = level_now * LOG_TWO * (1.0 - distance_slope)
    if level_now == 0:
        pair_len = 2 * BLOCK
        q_grp = q_now.reshape(row_count // pair_len, pair_len, width_all)
        k_grp = k_now.reshape(row_count // pair_len, pair_len, width_all)
        v_grp = v_now.reshape(row_count // pair_len, pair_len, width_all)
    else:
        q_grp = q_now.reshape(row_count // BLOCK, BLOCK, width_all)
        k_grp = k_now.reshape(row_count // (2 * BLOCK), 2, BLOCK, width_all)[:, ::-1].reshape(row_count // BLOCK, BLOCK, width_all)
        v_grp = v_now.reshape(row_count // (2 * BLOCK), 2, BLOCK, width_all)[:, ::-1].reshape(row_count // BLOCK, BLOCK, width_all)
    group_count = q_grp.shape[0]
    batch_len = min(group_count, 16)

    def run_batch(batch_args):
        return attend(batch_args[0], batch_args[1], batch_args[2], level_gain)
    shaped = tuple((member.reshape((group_count // batch_len, batch_len) + member.shape[1:]) for member in (q_grp, k_grp, v_grp)))
    row_max, numer, denom = lax.map(run_batch, shaped)
    head_count = distance_slope.shape[0]
    return (row_max.reshape(row_count, head_count), numer.reshape(row_count, width_all), denom.reshape(row_count, head_count))

def widen(level_stat, factor):
    return tuple((jnp.repeat(member, factor, axis=0) for member in level_stat))

def merge(earlier, latest):
    max_a, numer_a, denom_a = earlier
    max_b, numer_b, denom_b = latest
    row_max = jnp.maximum(max_a, max_b)
    scale_a = jnp.exp(max_a - row_max)
    scale_b = jnp.exp(max_b - row_max)
    row_count, width_all = numer_a.shape
    head_count = row_max.shape[1]
    numer = (numer_a.reshape(row_count, head_count, -1) * scale_a[:, :, None] + numer_b.reshape(row_count, head_count, -1) * scale_b[:, :, None]).reshape(row_count, width_all)
    denom = denom_a * scale_a + denom_b * scale_b
    return (row_max, numer, denom)

def reference(query_rows, key_rows, value_rows, distance_slope, out_weight):
    level_total = (TOKENS // BLOCK).bit_length() - 1
    q_now, k_now, v_now = (query_rows, key_rows, value_rows)
    combined = level_stats(q_now, k_now, v_now, 0, distance_slope)
    for level_now in range(1, level_total):
        q_now, k_now, v_now = (coarsen(q_now), coarsen(k_now), coarsen(v_now))
        far_stat = level_stats(q_now, k_now, v_now, level_now, distance_slope)
        combined = merge(combined, widen(far_stat, 2 ** level_now))
    row_max, numer, denom = combined
    row_count, width_all = numer.shape
    head_count = row_max.shape[1]
    attended = (numer.reshape(row_count, head_count, -1) / denom[:, :, None]).reshape(row_count, width_all).astype(jnp.bfloat16)
    return jnp.dot(attended, out_weight, preferred_element_type=jnp.float32).astype(jnp.bfloat16)
```

```python
import functools
import math

import jax
import jax.numpy as jnp
from jax import lax
from jax.experimental import pallas as pl
from jax.experimental.pallas import tpu as pltpu
from jax.sharding import PartitionSpec as P

BLOCK = 128
LANES = 128
LOG_TWO = math.log(2.0)
NEG = -1e30
BF = jnp.bfloat16
F32 = jnp.float32
MESH = pl.DeviceIdType.MESH


def rows_at(tokens, level):
    return max(16, tokens >> level)


def dot(a, b):
    return jnp.dot(a, b, preferred_element_type=F32)


def grid_ids(rows, cols):
    return (
        lax.broadcasted_iota(jnp.int32, (rows, cols), 0),
        lax.broadcasted_iota(jnp.int32, (rows, cols), 1),
    )


def pair_mean(rows, cols):
    r, c = grid_ids(rows, cols)
    return jnp.where(c // 2 == r, 0.5, 0.0).astype(BF)


def repeat_matrix(rows, cols):
    r, c = grid_ids(rows, cols)
    return jnp.where(r // 2 == c, 1.0, 0.0).astype(BF)


def stacked_mean(which):
    r, c = grid_ids(16, 16)
    if which == "key":
        hit = (r < 8) & (c // 2 == r)
    elif which == "value":
        hit = (r >= 8) & (c // 2 == r - 8)
    else:
        hit = ((r < 8) & (c < 8) & (c // 2 == r)) | (
            (r >= 8) & (c >= 8) & ((c - 8) // 2 == r - 8)
        )
    return jnp.where(hit, 0.5, 0.0).astype(BF)


def loop(count, body):
    if count <= 8:
        for k in range(count):
            body(k)
    else:

        def step(k, carry):
            body(k)
            return carry

        lax.fori_loop(0, count, step, 0)


def wait_bytes(ref, sem):
    pltpu.make_async_copy(ref, ref, sem).wait()


def attend(q, k, v, gains, coarse_ref, valid):
    rows = q.shape[0]
    keys = k.shape[0]
    left = lax.broadcasted_iota(jnp.int32, (1, LANES), 1) < LANES // 2
    zero = jnp.zeros_like(q)
    q2 = jnp.concatenate([jnp.where(left, q, zero), jnp.where(left, zero, q)], axis=0)
    s = lax.dot_general(q2, k, (((1,), (1,)), ((), ())), preferred_element_type=F32)
    if valid < 8:
        key_no = lax.broadcasted_iota(jnp.int32, (1, keys), 1)
        s = jnp.where(key_no % 8 < valid, s, NEG)
    top = jnp.max(s, axis=1, keepdims=True)
    if coarse_ref:
        row_no = lax.broadcasted_iota(jnp.int32, (2 * rows, 1), 0)
        gain = jnp.where(row_no < rows, gains[0], gains[1])
        top = (top + gain).astype(BF).astype(F32)
        p = jnp.exp(s - (top - gain)).astype(BF)
    else:
        p = jnp.exp(s - top).astype(BF)
    v_ones = jnp.concatenate([v, jnp.ones((keys, LANES), BF)], axis=1)
    o = dot(p, v_ones)
    top = jnp.broadcast_to(top, (2 * rows, LANES))
    pick = lambda x: jnp.where(left, x[:rows], x[rows:])
    return pick(top), pick(o[:, LANES:]), pick(o[:, :LANES])


def kernel(fine_n, coarse_n, tokens, width, heads, *refs):
    n_dev = fine_n * coarse_n
    chips = n_dev // 2
    last = n_dev.bit_length() - 1
    pairs = width // LANES
    half_w = width // 2
    zs = coarse_n // 2
    it = iter(refs)
    q_ref, k_ref, v_ref, slope_ref, w_ref, out_ref = (next(it) for _ in range(6))
    q_lv = [None] + [next(it) for _ in range(last)]
    own = [None] + [next(it) for _ in range(last)]
    sib = [None] + [next(it) for _ in range(last)]
    state = [next(it) for _ in range(last + 1)]
    wbuf = next(it)
    att = next(it)
    send_sem, recv_sem, fsend_sem, frecv_sem, wsend_sem, wrecv_sem = (next(it) for _ in range(6))

    f = lax.axis_index("fine")
    c = lax.axis_index("coarse")
    dev = c * fine_n + f
    core = f % 2
    chip = dev // 2
    z = c // 2
    y = c % 2
    cols = pl.ds(pl.multiple_of(core * half_w, LANES), half_w)

    def at(chip_no):
        d = chip_no * 2 + core
        return {"fine": d % fine_n, "coarse": d // fine_n}

    other_core = {"fine": f + 1 - 2 * core, "coarse": c}
    flip_y = {"fine": f, "coarse": c + 1 - 2 * y}

    wbuf[z, y] = w_ref[...]

    barrier = pltpu.get_barrier_semaphore()
    pl.semaphore_signal(barrier, inc=1, device_id=other_core, device_id_type=MESH)

    def greet(k):
        pl.semaphore_signal(
            barrier, inc=1, device_id=at((chip + k + 1) % chips), device_id_type=MESH
        )

    loop(chips - 1, greet)

    for level in range(1, last + 1):
        rows, prev = rows_at(tokens, level), rows_at(tokens, level - 1)
        mean = pair_mean(rows, prev)
        if level == 1:
            q_prev, k_prev, v_prev = q_ref[...] * jnp.asarray(0.125, BF), k_ref[...], v_ref[...]
        q_prev = dot(mean, q_prev).astype(BF)
        q_lv[level][...] = q_prev
        if tokens >> level >= 16:
            k_prev = dot(mean, k_prev).astype(BF)
            v_prev = dot(mean, v_prev).astype(BF)
            own[level][0] = k_prev
            own[level][1] = v_prev
        else:
            if tokens >> level == 8:
                both = dot(stacked_mean("key"), k_prev) + dot(stacked_mean("value"), v_prev)
            else:
                both = dot(stacked_mean("both"), both)
            both = both.astype(BF)
            own[level][...] = both

    pl.semaphore_wait(barrier, chips)

    def remote(src, dst, s_sem, r_sem, dev_id):
        return pltpu.make_async_remote_copy(
            src_ref=src, dst_ref=dst, send_sem=s_sem, recv_sem=r_sem,
            device_id=dev_id, device_id_type=MESH,
        )

    def w_first(k):
        z_to = (z + k + 1) % zs
        remote(
            w_ref.at[:, cols], wbuf.at[z, y, :, cols], wsend_sem.at[0], wrecv_sem.at[0],
            {"fine": f, "coarse": z_to * 2 + y},
        ).start()

    def half_of(level, which):
        if tokens >> level >= 16:
            return sib[level].at[:, pl.ds(pl.multiple_of(which * 64, 16), 64), :]
        n = sib[level].shape[0] // 2
        return sib[level].at[pl.ds(pl.multiple_of(which * n, 16), n), :]

    def send_level(level):
        group = 2 ** (level - 2)
        rows = rows_at(tokens, level)
        mine = chip % group
        g = chip // group
        base = (g + 1 - 2 * (g % 2)) * group

        if tokens >> level >= 16:
            start = pl.multiple_of(core * 64 + mine * rows, 16)
            dst = sib[level].at[:, pl.ds(start, rows), :]
        else:
            start = pl.multiple_of((core * group + mine) * 16, 16)
            dst = sib[level].at[pl.ds(start, 16), :]

        def one(k):
            to = base + (mine + k) % group
            remote(own[level], dst, send_sem.at[level], recv_sem.at[level], at(to)).start()

        loop(group, one)

    first = remote(own[1], sib[1], send_sem.at[1], recv_sem.at[1], other_core)
    first.start()
    for level in range(2, last + 1):
        send_level(level)
    loop(zs - 1, w_first)

    gain_of = lambda level, h: level * LOG_TWO * (1.0 - slope_ref[h])

    def run_level(level):
        rows = rows_at(tokens, level)
        valid = tokens >> level
        for p in range(pairs):
            cs = slice(p * LANES, (p + 1) * LANES)
            if level == 0:
                q = q_ref[:, cs] * jnp.asarray(0.125, BF)
                k, v = k_ref[:, cs], v_ref[:, cs]
            else:
                q = q_lv[level][:, cs]
                if valid >= 16:
                    k, v = sib[level][0, :, cs], sib[level][1, :, cs]
                else:
                    n = sib[level].shape[0] // 16
                    both = sib[level][:, cs].astype(F32).reshape(n, 2, 8, LANES)
                    k = both[:, 0].reshape(n * 8, LANES).astype(BF)
                    v = both[:, 1].reshape(n * 8, LANES).astype(BF)
            gains = (gain_of(level, 2 * p), gain_of(level, 2 * p + 1))
            m, den, num = attend(q, k, v, gains, level > 0, valid)
            state[level][0, :, cs] = m
            state[level][1, :, cs] = den
            state[level][2, :, cs] = num

    def forward(level):
        half = half_of(level, core)
        wait_bytes(half, recv_sem.at[level])
        remote(half, half, fsend_sem.at[level], frecv_sem.at[level], other_core).start()

    run_level(0)
    forward(2)
    first.wait_recv()
    run_level(1)
    for level in range(3, last + 1):
        forward(level)
    wait_bytes(wbuf.at[pl.ds(0, zs - 1), 0, :, cols], wrecv_sem.at[0])
    to_y = remote(
        wbuf.at[:, y, :, cols], wbuf.at[:, y, :, cols], wsend_sem.at[1], wrecv_sem.at[1], flip_y
    )
    to_y.start()
    for level in range(2, last + 1):
        wait_bytes(half_of(level, 1 - core), frecv_sem.at[level])
        run_level(level)
    to_y.wait_recv()
    to_core = remote(
        wbuf.at[:, :, :, cols], wbuf.at[:, :, :, cols], wsend_sem.at[2], wrecv_sem.at[2], other_core
    )
    to_core.start()

    def widen(e, m, den, num):
        def split(x):
            hi = x.astype(BF)
            lo = (x - hi.astype(F32)).astype(BF)
            return dot(e, hi) + dot(e, lo)

        return dot(e, m.astype(BF)), split(den), split(num)

    def merge(a, b):
        top = jnp.maximum(a[0], b[0])
        sa, sb = jnp.exp(a[0] - top), jnp.exp(b[0] - top)
        return top, a[1] * sa + b[1] * sb, a[2] * sa + b[2] * sb

    for p in range(pairs):
        cs = slice(p * LANES, (p + 1) * LANES)
        now = tuple(state[last][i, :, cs] for i in range(3))
        for level in range(last - 1, -1, -1):
            e = repeat_matrix(rows_at(tokens, level), rows_at(tokens, level + 1))
            now = merge(widen(e, *now), tuple(state[level][i, :, cs] for i in range(3)))
        att[:, cs] = (now[2] / now[1]).astype(BF)

    to_core.wait_recv()
    if wbuf.shape[2] % 16 == 0:
        w_all = wbuf[...].reshape(width, width)
    else:
        w_all = wbuf[...].astype(F32).reshape(width, width).astype(BF)
    out_ref[...] = dot(att[...], w_all).astype(BF)

    first.wait_send()
    for level in range(2, last + 1):
        half = half_of(level, core)
        wait_bytes(half, send_sem.at[level])
        wait_bytes(half, fsend_sem.at[level])
    wait_bytes(wbuf.at[pl.ds(0, zs - 1), 0, :, cols], wsend_sem.at[0])
    to_y.wait_send()
    to_core.wait_send()


def on_device(fine_n, coarse_n, query_rows, key_rows, value_rows, distance_slope, out_weight):
    tokens, width = query_rows.shape
    heads = distance_slope.shape[0]
    last = (fine_n * coarse_n).bit_length() - 1
    levels = range(1, last + 1)
    q_lv = [pltpu.VMEM((rows_at(tokens, l), width), BF) for l in levels]
    own, sib = [], []
    for l in levels:
        if tokens >> l >= 16:
            own.append(pltpu.VMEM((2, tokens >> l, width), BF))
            sib.append(pltpu.VMEM((2, BLOCK, width), BF))
        else:
            own.append(pltpu.VMEM((16, width), BF))
            sib.append(pltpu.VMEM((16 * 2 ** (l - 1), width), BF))
    state = [pltpu.VMEM((3, rows_at(tokens, l), width), F32) for l in range(last + 1)]
    dma = pltpu.SemaphoreType.DMA
    vmem = pl.BlockSpec(memory_space=pltpu.VMEM)
    return pl.pallas_call(
        functools.partial(kernel, fine_n, coarse_n, tokens, width, heads),
        out_shape=jax.ShapeDtypeStruct((tokens, width), BF),
        in_specs=[vmem, vmem, vmem, pl.BlockSpec(memory_space=pltpu.SMEM), vmem],
        out_specs=vmem,
        scratch_shapes=q_lv + own + sib + state + [
            pltpu.VMEM((coarse_n // 2, 2) + out_weight.shape, BF),
            pltpu.VMEM((tokens, width), BF),
            dma((last + 1,)), dma((last + 1,)), dma((last + 1,)), dma((last + 1,)),
            dma((3,)), dma((3,)),
        ],
        compiler_params=pltpu.CompilerParams(
            collective_id=0, has_side_effects=True, vmem_limit_bytes=48 * 2**20
        ),
        name="hierarchical_attention",
    )(query_rows, key_rows, value_rows, distance_slope, out_weight)


def solution(mesh):
    fine_n, coarse_n = mesh.shape["fine"], mesh.shape["coarse"]
    return jax.shard_map(
        functools.partial(on_device, fine_n, coarse_n),
        mesh=mesh,
        in_specs=(
            P(("coarse", "fine"), None),
            P(("coarse", "fine"), None),
            P(("coarse", "fine"), None),
            P(),
            P("coarse", None),
        ),
        out_specs=P(("coarse", "fine"), None),
        check_vma=False,
    )
```

```python
import functools
import math

import jax
import jax.numpy as jnp
from jax import lax
from jax.experimental import pallas as pl
from jax.experimental.pallas import tpu as pltpu
from jax.sharding import PartitionSpec as P

BLOCK = 128
LANES = 128
LOG_TWO = math.log(2.0)
NEG = -1e30
BF = jnp.bfloat16
F32 = jnp.float32
MESH = pl.DeviceIdType.MESH


def rows_at(tokens, level):
    return max(16, tokens >> level)


def dot(a, b):
    return jnp.dot(a, b, preferred_element_type=F32)


def grid_ids(rows, cols):
    return (
        lax.broadcasted_iota(jnp.int32, (rows, cols), 0),
        lax.broadcasted_iota(jnp.int32, (rows, cols), 1),
    )


def pair_mean(rows, cols):
    r, c = grid_ids(rows, cols)
    return jnp.where(c // 2 == r, 0.5, 0.0).astype(BF)


def repeat_matrix(rows, cols):
    r, c = grid_ids(rows, cols)
    return jnp.where(r // 2 == c, 1.0, 0.0).astype(BF)


def stacked_mean(which):
    r, c = grid_ids(16, 16)
    if which == "key":
        hit = (r < 8) & (c // 2 == r)
    elif which == "value":
        hit = (r >= 8) & (c // 2 == r - 8)
    else:
        hit = ((r < 8) & (c < 8) & (c // 2 == r)) | (
            (r >= 8) & (c >= 8) & ((c - 8) // 2 == r - 8)
        )
    return jnp.where(hit, 0.5, 0.0).astype(BF)


def loop(count, body):
    if count <= 8:
        for k in range(count):
            body(k)
    else:

        def step(k, carry):
            body(k)
            return carry

        lax.fori_loop(0, count, step, 0)


def wait_bytes(ref, sem):
    pltpu.make_async_copy(ref, ref, sem).wait()


def attend(q, k, v, gains, coarse_ref, valid):
    rows = q.shape[0]
    keys = k.shape[0]
    left = lax.broadcasted_iota(jnp.int32, (1, LANES), 1) < LANES // 2
    zero = jnp.zeros_like(q)
    q2 = jnp.concatenate([jnp.where(left, q, zero), jnp.where(left, zero, q)], axis=0)
    s = lax.dot_general(q2, k, (((1,), (1,)), ((), ())), preferred_element_type=F32)
    if valid < 8:
        key_no = lax.broadcasted_iota(jnp.int32, (1, keys), 1)
        s = jnp.where(key_no % 8 < valid, s, NEG)
    top = jnp.max(s, axis=1, keepdims=True)
    if coarse_ref:
        row_no = lax.broadcasted_iota(jnp.int32, (2 * rows, 1), 0)
        gain = jnp.where(row_no < rows, gains[0], gains[1])
        top = (top + gain).astype(BF).astype(F32)
        p = jnp.exp(s - (top - gain)).astype(BF)
    else:
        p = jnp.exp(s - top).astype(BF)
    v_ones = jnp.concatenate([v, jnp.ones((keys, LANES), BF)], axis=1)
    o = dot(p, v_ones)
    top = jnp.broadcast_to(top, (2 * rows, LANES))
    pick = lambda x: jnp.where(left, x[:rows], x[rows:])
    return pick(top), pick(o[:, LANES:]), pick(o[:, :LANES])


def kernel(fine_n, coarse_n, tokens, width, heads, *refs):
    n_dev = fine_n * coarse_n
    chips = n_dev // 2
    last = n_dev.bit_length() - 1
    pairs = width // LANES
    half_w = width // 2
    zs = coarse_n // 2
    it = iter(refs)
    q_hbm, k_hbm, v_hbm, slope_hbm, w_ref, out_ref = (next(it) for _ in range(6))
    q_ref, k_ref, v_ref, slope_ref = (next(it) for _ in range(4))
    q_lv = [None] + [next(it) for _ in range(last)]
    own = [None] + [next(it) for _ in range(last)]
    sib = [None] + [next(it) for _ in range(last)]
    state = [next(it) for _ in range(last + 1)]
    wbuf = next(it)
    att = next(it)
    send_sem, recv_sem, fsend_sem, frecv_sem = (next(it) for _ in range(4))
    load_sem, z_send, z_recv, y_send, y_recv, core_send, core_recv = (next(it) for _ in range(7))

    f = lax.axis_index("fine")
    c = lax.axis_index("coarse")
    dev = c * fine_n + f
    core = f % 2
    chip = dev // 2
    z = c // 2
    y = c % 2
    cols = pl.ds(pl.multiple_of(core * half_w, LANES), half_w)

    def at(chip_no):
        d = chip_no * 2 + core
        return {"fine": d % fine_n, "coarse": d // fine_n}

    other_core = {"fine": f + 1 - 2 * core, "coarse": c}
    flip_y = {"fine": f, "coarse": c + 1 - 2 * y}

    loads = [
        pltpu.make_async_copy(a, b, load_sem.at[i])
        for i, (a, b) in enumerate(
            (
                (k_hbm, k_ref),
                (v_hbm, v_ref),
                (q_hbm, q_ref),
                (w_ref.at[:, cols], wbuf.at[z, y, :, cols]),
                (slope_hbm, slope_ref),
            )
        )
    ]
    for load in loads:
        load.start()

    barrier = pltpu.get_barrier_semaphore()
    pl.semaphore_signal(barrier, inc=1, device_id=other_core, device_id_type=MESH)

    def greet(k):
        pl.semaphore_signal(
            barrier, inc=1, device_id=at((chip + k + 1) % chips), device_id_type=MESH
        )

    loop(chips - 1, greet)

    for load in loads:
        load.wait()

    for level in range(1, last + 1):
        rows, prev = rows_at(tokens, level), rows_at(tokens, level - 1)
        mean = pair_mean(rows, prev)
        if level == 1:
            q_prev, k_prev, v_prev = q_ref[...] * jnp.asarray(0.125, BF), k_ref[...], v_ref[...]
        q_prev = dot(mean, q_prev).astype(BF)
        q_lv[level][...] = q_prev
        if tokens >> level >= 16:
            k_prev = dot(mean, k_prev).astype(BF)
            v_prev = dot(mean, v_prev).astype(BF)
            own[level][0] = k_prev
            own[level][1] = v_prev
        else:
            if tokens >> level == 8:
                both = dot(stacked_mean("key"), k_prev) + dot(stacked_mean("value"), v_prev)
            else:
                both = dot(stacked_mean("both"), both)
            both = both.astype(BF)
            own[level][...] = both

    pl.semaphore_wait(barrier, chips)

    def remote(src, dst, s_sem, r_sem, dev_id):
        return pltpu.make_async_remote_copy(
            src_ref=src, dst_ref=dst, send_sem=s_sem, recv_sem=r_sem,
            device_id=dev_id, device_id_type=MESH,
        )

    def w_first(k):
        z_to = (z + k + 1) % zs
        remote(
            wbuf.at[z, y, :, cols], wbuf.at[z, y, :, cols], z_send.at[k], z_recv.at[k],
            {"fine": f, "coarse": z_to * 2 + y},
        ).start()

    def w_second(k, z_from):
        part = wbuf.at[z_from, y, :, cols]
        remote(part, part, y_send.at[k], y_recv.at[k], flip_y).start()

    def w_pass(k):
        z_from = (z - (k + 1) + zs) % zs
        wait_bytes(wbuf.at[z_from, y, :, cols], z_recv.at[k])
        w_second(k + 1, z_from)

    def half_of(level, which):
        if tokens >> level >= 16:
            return sib[level].at[:, pl.ds(pl.multiple_of(which * 64, 16), 64), :]
        n = sib[level].shape[0] // 2
        return sib[level].at[pl.ds(pl.multiple_of(which * n, 16), n), :]

    def send_level(level):
        group = 2 ** (level - 2)
        rows = rows_at(tokens, level)
        mine = chip % group
        g = chip // group
        base = (g + 1 - 2 * (g % 2)) * group

        if tokens >> level >= 16:
            start = pl.multiple_of(core * 64 + mine * rows, 16)
            dst = sib[level].at[:, pl.ds(start, rows), :]
        else:
            start = pl.multiple_of((core * group + mine) * 16, 16)
            dst = sib[level].at[pl.ds(start, 16), :]

        def one(k):
            to = base + (mine + k) % group
            remote(own[level], dst, send_sem.at[level], recv_sem.at[level], at(to)).start()

        loop(group, one)

    w_second(0, z)
    loop(zs - 1, w_first)
    first = remote(own[1], sib[1], send_sem.at[1], recv_sem.at[1], other_core)
    first.start()
    for level in range(2, last + 1):
        send_level(level)

    gain_of = lambda level, h: level * LOG_TWO * (1.0 - slope_ref[h])

    def run_level(level):
        rows = rows_at(tokens, level)
        valid = tokens >> level
        for p in range(pairs):
            cs = slice(p * LANES, (p + 1) * LANES)
            if level == 0:
                q = q_ref[:, cs] * jnp.asarray(0.125, BF)
                k, v = k_ref[:, cs], v_ref[:, cs]
            else:
                q = q_lv[level][:, cs]
                if valid >= 16:
                    k, v = sib[level][0, :, cs], sib[level][1, :, cs]
                else:
                    n = sib[level].shape[0] // 16
                    both = sib[level][:, cs].astype(F32).reshape(n, 2, 8, LANES)
                    k = both[:, 0].reshape(n * 8, LANES).astype(BF)
                    v = both[:, 1].reshape(n * 8, LANES).astype(BF)
            gains = (gain_of(level, 2 * p), gain_of(level, 2 * p + 1))
            m, den, num = attend(q, k, v, gains, level > 0, valid)
            state[level][0, :, cs] = m
            state[level][1, :, cs] = den
            state[level][2, :, cs] = num

    def forward(level):
        half = half_of(level, core)
        wait_bytes(half, recv_sem.at[level])
        remote(half, half, fsend_sem.at[level], frecv_sem.at[level], other_core).start()

    def w_third(which):
        part = wbuf.at[:, which, :, cols]
        copy = remote(part, part, core_send.at[which], core_recv.at[which], other_core)
        copy.start()

    run_level(0)
    forward(2)
    first.wait_recv()
    run_level(1)
    loop(zs - 1, w_pass)
    w_third(y)
    for level in range(3, last + 1):
        forward(level)
    for level in range(2, last + 1):
        wait_bytes(half_of(level, 1 - core), frecv_sem.at[level])
        run_level(level)
    loop(zs, lambda k: wait_bytes(wbuf.at[(z - k + zs) % zs, 1 - y, :, cols], y_recv.at[k]))
    w_third(1 - y)

    def widen(e, m, den, num):
        def split(x):
            hi = x.astype(BF)
            lo = (x - hi.astype(F32)).astype(BF)
            return dot(e, hi) + dot(e, lo)

        return dot(e, m.astype(BF)), split(den), split(num)

    def merge(a, b):
        top = jnp.maximum(a[0], b[0])
        sa, sb = jnp.exp(a[0] - top), jnp.exp(b[0] - top)
        return top, a[1] * sa + b[1] * sb, a[2] * sa + b[2] * sb

    for p in range(pairs):
        cs = slice(p * LANES, (p + 1) * LANES)
        now = tuple(state[last][i, :, cs] for i in range(3))
        for level in range(last - 1, -1, -1):
            e = repeat_matrix(rows_at(tokens, level), rows_at(tokens, level + 1))
            now = merge(widen(e, *now), tuple(state[level][i, :, cs] for i in range(3)))
        att[:, cs] = (now[2] / now[1]).astype(BF)

    other_cols = pl.ds(pl.multiple_of((1 - core) * half_w, LANES), half_w)
    for i in range(2):
        wait_bytes(wbuf.at[:, i, :, other_cols], core_recv.at[i])
    if wbuf.shape[2] % 16 == 0:
        w_all = wbuf[...].reshape(width, width)
    else:
        w_all = wbuf[...].astype(F32).reshape(width, width).astype(BF)
    out_ref[...] = dot(att[...], w_all).astype(BF)

    first.wait_send()
    for level in range(2, last + 1):
        half = half_of(level, core)
        wait_bytes(half, send_sem.at[level])
        wait_bytes(half, fsend_sem.at[level])
    part = wbuf.at[z, y, :, cols]
    loop(zs - 1, lambda k: wait_bytes(part, z_send.at[k]))
    loop(zs, lambda k: wait_bytes(part, y_send.at[k]))
    for i in range(2):
        wait_bytes(wbuf.at[:, i, :, cols], core_send.at[i])


def on_device(fine_n, coarse_n, query_rows, key_rows, value_rows, distance_slope, out_weight):
    tokens, width = query_rows.shape
    heads = distance_slope.shape[0]
    last = (fine_n * coarse_n).bit_length() - 1
    levels = range(1, last + 1)
    q_lv = [pltpu.VMEM((rows_at(tokens, l), width), BF) for l in levels]
    own, sib = [], []
    for l in levels:
        if tokens >> l >= 16:
            own.append(pltpu.VMEM((2, tokens >> l, width), BF))
            sib.append(pltpu.VMEM((2, BLOCK, width), BF))
        else:
            own.append(pltpu.VMEM((16, width), BF))
            sib.append(pltpu.VMEM((16 * 2 ** (l - 1), width), BF))
    state = [pltpu.VMEM((3, rows_at(tokens, l), width), F32) for l in range(last + 1)]
    dma = pltpu.SemaphoreType.DMA
    zs = coarse_n // 2
    vmem = pl.BlockSpec(memory_space=pltpu.VMEM)
    return pl.pallas_call(
        functools.partial(kernel, fine_n, coarse_n, tokens, width, heads),
        out_shape=jax.ShapeDtypeStruct((tokens, width), BF),
        in_specs=[pl.BlockSpec(memory_space=pltpu.HBM)] * 5,
        out_specs=vmem,
        scratch_shapes=[pltpu.VMEM((tokens, width), BF)] * 3 + [pltpu.SMEM((heads,), F32)] + q_lv + own + sib + state + [
            pltpu.VMEM((coarse_n // 2, 2) + out_weight.shape, BF),
            pltpu.VMEM((tokens, width), BF),
            dma((last + 1,)), dma((last + 1,)), dma((last + 1,)), dma((last + 1,)),
            dma((5,)), dma((zs,)), dma((zs,)), dma((zs,)), dma((zs,)), dma((2,)), dma((2,)),
        ],
        compiler_params=pltpu.CompilerParams(
            collective_id=0, has_side_effects=True, vmem_limit_bytes=62 * 2**20
        ),
        name="hierarchical_attention",
    )(query_rows, key_rows, value_rows, distance_slope, out_weight)


def solution(mesh):
    fine_n, coarse_n = mesh.shape["fine"], mesh.shape["coarse"]
    return jax.shard_map(
        functools.partial(on_device, fine_n, coarse_n),
        mesh=mesh,
        in_specs=(
            P(("coarse", "fine"), None),
            P(("coarse", "fine"), None),
            P(("coarse", "fine"), None),
            P(),
            P("coarse", None),
        ),
        out_specs=P(("coarse", "fine"), None),
        check_vma=False,
    )
```

```python
import functools
import math

import jax
import jax.numpy as jnp
from jax import lax
from jax.experimental import pallas as pl
from jax.experimental.pallas import tpu as pltpu
from jax.sharding import PartitionSpec as P

BLOCK = 128
LANES = 128
LOG_TWO = math.log(2.0)
NEG = -1e30
BF = jnp.bfloat16
F32 = jnp.float32
MESH = pl.DeviceIdType.MESH


def rows_at(tokens, level):
    return max(16, tokens >> level)


def dot(a, b):
    return jnp.dot(a, b, preferred_element_type=F32)


def grid_ids(rows, cols):
    return (
        lax.broadcasted_iota(jnp.int32, (rows, cols), 0),
        lax.broadcasted_iota(jnp.int32, (rows, cols), 1),
    )


def pair_mean(rows, cols):
    r, c = grid_ids(rows, cols)
    return jnp.where(c // 2 == r, 0.5, 0.0).astype(BF)


def repeat_matrix(rows, cols):
    r, c = grid_ids(rows, cols)
    return jnp.where(r // 2 == c, 1.0, 0.0).astype(BF)


def stacked_mean(which):
    r, c = grid_ids(16, 16)
    if which == "key":
        hit = (r < 8) & (c // 2 == r)
    elif which == "value":
        hit = (r >= 8) & (c // 2 == r - 8)
    else:
        hit = ((r < 8) & (c < 8) & (c // 2 == r)) | (
            (r >= 8) & (c >= 8) & ((c - 8) // 2 == r - 8)
        )
    return jnp.where(hit, 0.5, 0.0).astype(BF)


def loop(count, body):
    if count <= 8:
        for k in range(count):
            body(k)
    else:

        def step(k, carry):
            body(k)
            return carry

        lax.fori_loop(0, count, step, 0)


def wait_bytes(ref, sem):
    pltpu.make_async_copy(ref, ref, sem).wait()


def attend(q, k, v, gains, coarse_ref, valid):
    rows = q.shape[0]
    keys = k.shape[0]
    left = lax.broadcasted_iota(jnp.int32, (1, LANES), 1) < LANES // 2
    zero = jnp.zeros_like(q)
    q2 = jnp.concatenate([jnp.where(left, q, zero), jnp.where(left, zero, q)], axis=0)
    s = lax.dot_general(q2, k, (((1,), (1,)), ((), ())), preferred_element_type=F32)
    if valid < 8:
        key_no = lax.broadcasted_iota(jnp.int32, (1, keys), 1)
        s = jnp.where(key_no % 8 < valid, s, NEG)
    top = jnp.max(s, axis=1, keepdims=True)
    if coarse_ref:
        row_no = lax.broadcasted_iota(jnp.int32, (2 * rows, 1), 0)
        gain = jnp.where(row_no < rows, gains[0], gains[1])
        top = (top + gain).astype(BF).astype(F32)
        p = jnp.exp(s - (top - gain)).astype(BF)
    else:
        p = jnp.exp(s - top).astype(BF)
    v_ones = jnp.concatenate([v, jnp.ones((keys, LANES), BF)], axis=1)
    o = dot(p, v_ones)
    top = jnp.broadcast_to(top, (2 * rows, LANES))
    pick = lambda x: jnp.where(left, x[:rows], x[rows:])
    return pick(top), pick(o[:, LANES:]), pick(o[:, :LANES])


def kernel(fine_n, coarse_n, tokens, width, heads, *refs):
    n_dev = fine_n * coarse_n
    fine_bits = fine_n.bit_length() - 2
    last = n_dev.bit_length() - 1
    pairs = width // LANES
    half_w = width // 2
    zs = coarse_n // 2
    it = iter(refs)
    q_hbm, k_hbm, v_hbm, slope_hbm, w_ref, out_ref = (next(it) for _ in range(6))
    q_ref, k_ref, v_ref, slope_ref = (next(it) for _ in range(4))
    q_lv = [None] + [next(it) for _ in range(last)]
    own = [None] + [next(it) for _ in range(last)]
    sib = [None] + [next(it) for _ in range(last)]
    state = [next(it) for _ in range(last + 1)]
    wbuf = next(it)
    att = next(it)
    send_sem, recv_sem, fsend_sem, frecv_sem = (next(it) for _ in range(4))
    load_sem, z_send, z_recv, y_send, y_recv, core_send, core_recv = (next(it) for _ in range(7))

    f = lax.axis_index("fine")
    c = lax.axis_index("coarse")
    dev = c * fine_n + f
    core = f % 2
    chip = dev // 2
    z = c // 2
    y = c % 2
    cols = pl.ds(pl.multiple_of(core * half_w, LANES), half_w)

    def at(chip_no):
        d = chip_no * 2 + core
        return {"fine": d % fine_n, "coarse": d // fine_n}

    def flip(bit):
        return chip + (1 - 2 * (chip // 2**bit % 2)) * 2**bit

    other_core = {"fine": f + 1 - 2 * core, "coarse": c}
    flip_y = {"fine": f, "coarse": c + 1 - 2 * y}

    loads = [
        pltpu.make_async_copy(a, b, load_sem.at[i])
        for i, (a, b) in enumerate(
            (
                (k_hbm, k_ref),
                (v_hbm, v_ref),
                (q_hbm, q_ref),
                (w_ref.at[:, cols], wbuf.at[z, y, :, cols]),
                (slope_hbm, slope_ref),
            )
        )
    ]
    for load in loads:
        load.start()

    barrier = pltpu.get_barrier_semaphore()
    pl.semaphore_signal(barrier, inc=1, device_id=other_core, device_id_type=MESH)

    pl.semaphore_signal(barrier, inc=1, device_id=flip_y, device_id_type=MESH)
    for bit in range(fine_bits):
        pl.semaphore_signal(barrier, inc=1, device_id=at(flip(bit)), device_id_type=MESH)

    def greet(k):
        peer = {"fine": f, "coarse": (z + k + 1) % zs * 2 + y}
        pl.semaphore_signal(barrier, inc=1, device_id=peer, device_id_type=MESH)

    loop(zs - 1, greet)

    for load in loads:
        load.wait()

    for level in range(1, last + 1):
        rows, prev = rows_at(tokens, level), rows_at(tokens, level - 1)
        mean = pair_mean(rows, prev)
        if level == 1:
            q_prev, k_prev, v_prev = q_ref[...] * jnp.asarray(0.125, BF), k_ref[...], v_ref[...]
        q_prev = dot(mean, q_prev).astype(BF)
        q_lv[level][...] = q_prev
        if tokens >> level >= 16:
            k_prev = dot(mean, k_prev).astype(BF)
            v_prev = dot(mean, v_prev).astype(BF)
            own[level][0] = k_prev
            own[level][1] = v_prev
        else:
            if tokens >> level == 8:
                both = dot(stacked_mean("key"), k_prev) + dot(stacked_mean("value"), v_prev)
            else:
                both = dot(stacked_mean("both"), both)
            both = both.astype(BF)
            own[level][...] = both

    pl.semaphore_wait(barrier, 1 + fine_bits + zs)

    def remote(src, dst, s_sem, r_sem, dev_id):
        return pltpu.make_async_remote_copy(
            src_ref=src, dst_ref=dst, send_sem=s_sem, recv_sem=r_sem,
            device_id=dev_id, device_id_type=MESH,
        )

    def w_first(k):
        z_to = (z + k + 1) % zs
        remote(
            wbuf.at[z, y, :, cols], wbuf.at[z, y, :, cols], z_send.at[k], z_recv.at[k],
            {"fine": f, "coarse": z_to * 2 + y},
        ).start()

    def w_second(k, z_from):
        part = wbuf.at[z_from, y, :, cols]
        remote(part, part, y_send.at[k], y_recv.at[k], flip_y).start()

    def w_pass(k):
        z_from = (z - (k + 1) + zs) % zs
        wait_bytes(wbuf.at[z_from, y, :, cols], z_recv.at[k])
        w_second(k + 1, z_from)

    def half_of(level, which):
        if tokens >> level >= 16:
            return sib[level].at[:, pl.ds(pl.multiple_of(which * 64, 16), 64), :]
        n = sib[level].shape[0] // 2
        return sib[level].at[pl.ds(pl.multiple_of(which * n, 16), n), :]

    def block_of(level, start, count):
        group = 2 ** (level - 2)
        if tokens >> level >= 16:
            rows = tokens >> level
            at_row = pl.multiple_of(core * 64 + start * rows, 16)
            return sib[level].at[:, pl.ds(at_row, rows * count), :]
        return sib[level].at[pl.ds(pl.multiple_of((core * group + start) * 16, 16), 16 * count), :]

    def piece(level, step):
        group = 2 ** (level - 2)
        mine = chip % group
        if step == 0:
            here = block_of(level, mine, 1)
            return own[level], here, level - 2, here
        width_b = 2 ** (step - 1)
        n = mine // width_b
        here = block_of(level, n * width_b, width_b)
        there = block_of(level, (n + 1 - 2 * (n % 2)) * width_b, width_b)
        return here, here, step - 1, there

    def exchange(step):
        for level in range(max(2, step + 1), last + 1):
            if step >= 1:
                got = piece(level, step - 1)[3]
                wait_bytes(got, recv_sem.at[level * last + step - 1])
            if step <= level - 2:
                src, dst, bit, _ = piece(level, step)
                sem = level * last + step
                remote(src, dst, send_sem.at[sem], recv_sem.at[sem], at(flip(bit))).start()
            else:
                half = half_of(level, core)
                remote(half, half, fsend_sem.at[level], frecv_sem.at[level], other_core).start()

    first = remote(own[1], sib[1], send_sem.at[1], recv_sem.at[1], other_core)
    first.start()
    exchange(0)
    w_second(0, z)
    loop(zs - 1, w_first)

    gain_of = lambda level, h: level * LOG_TWO * (1.0 - slope_ref[h])

    def run_level(level, between=None):
        rows = rows_at(tokens, level)
        valid = tokens >> level
        for p in range(pairs):
            cs = slice(p * LANES, (p + 1) * LANES)
            if level == 0:
                q = q_ref[:, cs] * jnp.asarray(0.125, BF)
                k, v = k_ref[:, cs], v_ref[:, cs]
            else:
                q = q_lv[level][:, cs]
                if valid >= 16:
                    k, v = sib[level][0, :, cs], sib[level][1, :, cs]
                else:
                    n = sib[level].shape[0] // 16
                    both = sib[level][:, cs].astype(F32).reshape(n, 2, 8, LANES)
                    k = both[:, 0].reshape(n * 8, LANES).astype(BF)
                    v = both[:, 1].reshape(n * 8, LANES).astype(BF)
            gains = (gain_of(level, 2 * p), gain_of(level, 2 * p + 1))
            m, den, num = attend(q, k, v, gains, level > 0, valid)
            state[level][0, :, cs] = m
            state[level][1, :, cs] = den
            state[level][2, :, cs] = num
            if between is not None:
                between(p)

    def w_third(which):
        part = wbuf.at[:, which, :, cols]
        copy = remote(part, part, core_send.at[which], core_recv.at[which], other_core)
        copy.start()

    def rounds(p):
        if p % 2 == 1 and p // 2 + 1 < last:
            exchange(p // 2 + 1)

    run_level(0, rounds)
    first.wait_recv()
    for step in range(pairs // 2 + 1, last):
        exchange(step)
    run_level(1)
    loop(zs - 1, w_pass)
    w_third(y)
    for level in range(2, last + 1):
        wait_bytes(half_of(level, 1 - core), frecv_sem.at[level])
        run_level(level)
    loop(zs, lambda k: wait_bytes(wbuf.at[(z - k + zs) % zs, 1 - y, :, cols], y_recv.at[k]))
    w_third(1 - y)

    def widen(e, m, den, num):
        def split(x):
            hi = x.astype(BF)
            lo = (x - hi.astype(F32)).astype(BF)
            return dot(e, hi) + dot(e, lo)

        return dot(e, m.astype(BF)), split(den), split(num)

    def merge(a, b):
        top = jnp.maximum(a[0], b[0])
        sa, sb = jnp.exp(a[0] - top), jnp.exp(b[0] - top)
        return top, a[1] * sa + b[1] * sb, a[2] * sa + b[2] * sb

    for p in range(pairs):
        cs = slice(p * LANES, (p + 1) * LANES)
        now = tuple(state[last][i, :, cs] for i in range(3))
        for level in range(last - 1, -1, -1):
            e = repeat_matrix(rows_at(tokens, level), rows_at(tokens, level + 1))
            now = merge(widen(e, *now), tuple(state[level][i, :, cs] for i in range(3)))
        att[:, cs] = (now[2] / now[1]).astype(BF)

    other_cols = pl.ds(pl.multiple_of((1 - core) * half_w, LANES), half_w)
    for i in range(2):
        wait_bytes(wbuf.at[:, i, :, other_cols], core_recv.at[i])
    if wbuf.shape[2] % 16 == 0:
        w_all = wbuf[...].reshape(width, width)
    else:
        w_all = wbuf[...].astype(F32).reshape(width, width).astype(BF)
    out_ref[...] = dot(att[...], w_all).astype(BF)

    first.wait_send()
    for level in range(2, last + 1):
        half = half_of(level, core)
        for step in range(level - 1):
            wait_bytes(piece(level, step)[0], send_sem.at[level * last + step])
        wait_bytes(half, fsend_sem.at[level])
    part = wbuf.at[z, y, :, cols]
    loop(zs - 1, lambda k: wait_bytes(part, z_send.at[k]))
    loop(zs, lambda k: wait_bytes(part, y_send.at[k]))
    for i in range(2):
        wait_bytes(wbuf.at[:, i, :, cols], core_send.at[i])


def on_device(fine_n, coarse_n, query_rows, key_rows, value_rows, distance_slope, out_weight):
    tokens, width = query_rows.shape
    heads = distance_slope.shape[0]
    last = (fine_n * coarse_n).bit_length() - 1
    levels = range(1, last + 1)
    q_lv = [pltpu.VMEM((rows_at(tokens, l), width), BF) for l in levels]
    own, sib = [], []
    for l in levels:
        if tokens >> l >= 16:
            own.append(pltpu.VMEM((2, tokens >> l, width), BF))
            sib.append(pltpu.VMEM((2, BLOCK, width), BF))
        else:
            own.append(pltpu.VMEM((16, width), BF))
            sib.append(pltpu.VMEM((16 * 2 ** (l - 1), width), BF))
    state = [pltpu.VMEM((3, rows_at(tokens, l), width), F32) for l in range(last + 1)]
    dma = pltpu.SemaphoreType.DMA
    zs = coarse_n // 2
    vmem = pl.BlockSpec(memory_space=pltpu.VMEM)
    return pl.pallas_call(
        functools.partial(kernel, fine_n, coarse_n, tokens, width, heads),
        out_shape=jax.ShapeDtypeStruct((tokens, width), BF),
        in_specs=[pl.BlockSpec(memory_space=pltpu.HBM)] * 5,
        out_specs=vmem,
        scratch_shapes=[pltpu.VMEM((tokens, width), BF)] * 3 + [pltpu.SMEM((heads,), F32)] + q_lv + own + sib + state + [
            pltpu.VMEM((coarse_n // 2, 2) + out_weight.shape, BF),
            pltpu.VMEM((tokens, width), BF),
            dma(((last + 1) * last,)), dma(((last + 1) * last,)), dma((last + 1,)), dma((last + 1,)),
            dma((5,)), dma((zs,)), dma((zs,)), dma((zs,)), dma((zs,)), dma((2,)), dma((2,)),
        ],
        compiler_params=pltpu.CompilerParams(
            collective_id=0, has_side_effects=True, vmem_limit_bytes=62 * 2**20
        ),
        name="hierarchical_attention",
    )(query_rows, key_rows, value_rows, distance_slope, out_weight)


def solution(mesh):
    fine_n, coarse_n = mesh.shape["fine"], mesh.shape["coarse"]
    return jax.shard_map(
        functools.partial(on_device, fine_n, coarse_n),
        mesh=mesh,
        in_specs=(
            P(("coarse", "fine"), None),
            P(("coarse", "fine"), None),
            P(("coarse", "fine"), None),
            P(),
            P("coarse", None),
        ),
        out_specs=P(("coarse", "fine"), None),
        check_vma=False,
    )
```

```python
import functools
import math

import jax
import jax.numpy as jnp
from jax import lax
from jax.experimental import pallas as pl
from jax.experimental.pallas import tpu as pltpu
from jax.sharding import PartitionSpec as P

BLOCK = 128
LANES = 128
LOG_TWO = math.log(2.0)
NEG = -1e30
BF = jnp.bfloat16
F32 = jnp.float32
MESH = pl.DeviceIdType.MESH


def rows_at(tokens, level):
    return max(16, tokens >> level)


def dot(a, b):
    return jnp.dot(a, b, preferred_element_type=F32)


def grid_ids(rows, cols):
    return (
        lax.broadcasted_iota(jnp.int32, (rows, cols), 0),
        lax.broadcasted_iota(jnp.int32, (rows, cols), 1),
    )


def pair_mean(rows, cols):
    r, c = grid_ids(rows, cols)
    return jnp.where(c // 2 == r, 0.5, 0.0).astype(BF)


def repeat_matrix(rows, cols):
    r, c = grid_ids(rows, cols)
    return jnp.where(r // 2 == c, 1.0, 0.0).astype(BF)


def stacked_mean(which):
    r, c = grid_ids(16, 16)
    if which == "key":
        hit = (r < 8) & (c // 2 == r)
    elif which == "value":
        hit = (r >= 8) & (c // 2 == r - 8)
    else:
        hit = ((r < 8) & (c < 8) & (c // 2 == r)) | (
            (r >= 8) & (c >= 8) & ((c - 8) // 2 == r - 8)
        )
    return jnp.where(hit, 0.5, 0.0).astype(BF)


def loop(count, body):
    if count <= 8:
        for k in range(count):
            body(k)
    else:

        def step(k, carry):
            body(k)
            return carry

        lax.fori_loop(0, count, step, 0)


def wait_bytes(ref, sem):
    pltpu.make_async_copy(ref, ref, sem).wait()


def head_scores(q, k):
    left = lax.broadcasted_iota(jnp.int32, (1, LANES), 1) < LANES // 2
    zero = jnp.zeros_like(q)
    q2 = jnp.concatenate([jnp.where(left, q, zero), jnp.where(left, zero, q)], axis=0)
    return lax.dot_general(q2, k, (((1,), (1,)), ((), ())), preferred_element_type=F32)


def head_weights(s, gains, coarse_ref, valid):
    if valid < 8:
        key_no = lax.broadcasted_iota(jnp.int32, (1, s.shape[1]), 1)
        s = jnp.where(key_no % 8 < valid, s, NEG)
    top = jnp.max(s, axis=1, keepdims=True)
    if not coarse_ref:
        return top, jnp.exp(s - top).astype(BF)
    rows = s.shape[0] // 2
    row_no = lax.broadcasted_iota(jnp.int32, (2 * rows, 1), 0)
    gain = jnp.where(row_no < rows, gains[0], gains[1])
    top = (top + gain).astype(BF).astype(F32)
    return top, jnp.exp(s - (top - gain)).astype(BF)


def head_sums(top, p, v):
    rows = p.shape[0] // 2
    left = lax.broadcasted_iota(jnp.int32, (1, LANES), 1) < LANES // 2
    o = dot(p, jnp.concatenate([v, jnp.ones(v.shape, BF)], axis=1))
    top = jnp.broadcast_to(top, (2 * rows, LANES))
    pick = lambda x: jnp.where(left, x[:rows], x[rows:])
    return pick(top), pick(o[:, LANES:]), pick(o[:, :LANES])


def kernel(fine_n, coarse_n, tokens, width, heads, *refs):
    n_dev = fine_n * coarse_n
    chips = n_dev // 2
    last = n_dev.bit_length() - 1
    pairs = width // LANES
    half_w = width // 2
    zs = coarse_n // 2
    it = iter(refs)
    q_hbm, k_hbm, v_hbm, slope_hbm, w_ref, out_ref = (next(it) for _ in range(6))
    q_ref, k_ref, v_ref, slope_ref = (next(it) for _ in range(4))
    q_lv = [None] + [next(it) for _ in range(last)]
    own = [None] + [next(it) for _ in range(last)]
    sib = [None] + [next(it) for _ in range(last)]
    state = [next(it) for _ in range(last + 1)]
    wbuf = next(it)
    att = next(it)
    send_sem, recv_sem, fsend_sem, frecv_sem = (next(it) for _ in range(4))
    load_sem, z_send, z_recv, y_send, y_recv, core_send, core_recv = (next(it) for _ in range(7))

    f = lax.axis_index("fine")
    c = lax.axis_index("coarse")
    dev = c * fine_n + f
    core = f % 2
    chip = dev // 2
    z = c // 2
    y = c % 2
    cols = pl.ds(pl.multiple_of(core * half_w, LANES), half_w)

    def at(chip_no):
        d = chip_no * 2 + core
        return {"fine": d % fine_n, "coarse": d // fine_n}

    other_core = {"fine": f + 1 - 2 * core, "coarse": c}
    flip_y = {"fine": f, "coarse": c + 1 - 2 * y}

    loads = [
        pltpu.make_async_copy(a, b, load_sem.at[i])
        for i, (a, b) in enumerate(
            (
                (k_hbm, k_ref),
                (v_hbm, v_ref),
                (q_hbm, q_ref),
                (w_ref.at[:, cols], wbuf.at[z, y, :, cols]),
                (slope_hbm, slope_ref),
            )
        )
    ]
    for load in loads:
        load.start()

    barrier = pltpu.get_barrier_semaphore()
    pl.semaphore_signal(barrier, inc=1, device_id=other_core, device_id_type=MESH)

    def greet(k):
        pl.semaphore_signal(
            barrier, inc=1, device_id=at((chip + k + 1) % chips), device_id_type=MESH
        )

    loop(chips - 1, greet)

    for load in loads:
        load.wait()

    for level in range(1, last + 1):
        rows, prev = rows_at(tokens, level), rows_at(tokens, level - 1)
        mean = pair_mean(rows, prev)
        if level == 1:
            q_prev, k_prev, v_prev = q_ref[...] * jnp.asarray(0.125, BF), k_ref[...], v_ref[...]
        q_prev = dot(mean, q_prev).astype(BF)
        q_lv[level][...] = q_prev
        if tokens >> level >= 16:
            k_prev = dot(mean, k_prev).astype(BF)
            v_prev = dot(mean, v_prev).astype(BF)
            own[level][0] = k_prev
            own[level][1] = v_prev
        else:
            if tokens >> level == 8:
                both = dot(stacked_mean("key"), k_prev) + dot(stacked_mean("value"), v_prev)
            else:
                both = dot(stacked_mean("both"), both)
            both = both.astype(BF)
            own[level][...] = both

    pl.semaphore_wait(barrier, chips)

    def remote(src, dst, s_sem, r_sem, dev_id):
        return pltpu.make_async_remote_copy(
            src_ref=src, dst_ref=dst, send_sem=s_sem, recv_sem=r_sem,
            device_id=dev_id, device_id_type=MESH,
        )

    def w_first(k):
        z_to = (z + k + 1) % zs
        remote(
            wbuf.at[z, y, :, cols], wbuf.at[z, y, :, cols], z_send.at[k], z_recv.at[k],
            {"fine": f, "coarse": z_to * 2 + y},
        ).start()

    def w_second(k, z_from):
        part = wbuf.at[z_from, y, :, cols]
        remote(part, part, y_send.at[k], y_recv.at[k], flip_y).start()

    def w_pass(k):
        z_from = (z - (k + 1) + zs) % zs
        wait_bytes(wbuf.at[z_from, y, :, cols], z_recv.at[k])
        w_second(k + 1, z_from)

    def half_of(level, which):
        if tokens >> level >= 16:
            return sib[level].at[:, pl.ds(pl.multiple_of(which * 64, 16), 64), :]
        n = sib[level].shape[0] // 2
        return sib[level].at[pl.ds(pl.multiple_of(which * n, 16), n), :]

    def send_level(level):
        group = 2 ** (level - 2)
        rows = rows_at(tokens, level)
        mine = chip % group
        g = chip // group
        base = (g + 1 - 2 * (g % 2)) * group

        if tokens >> level >= 16:
            start = pl.multiple_of(core * 64 + mine * rows, 16)
            dst = sib[level].at[:, pl.ds(start, rows), :]
        else:
            start = pl.multiple_of((core * group + mine) * 16, 16)
            dst = sib[level].at[pl.ds(start, 16), :]

        def one(k):
            to = base + (mine + k) % group
            remote(own[level], dst, send_sem.at[level], recv_sem.at[level], at(to)).start()

        loop(group, one)

    w_second(0, z)
    loop(zs - 1, w_first)
    first = remote(own[1], sib[1], send_sem.at[1], recv_sem.at[1], other_core)
    first.start()
    for level in range(2, last + 1):
        send_level(level)

    gain_of = lambda level, h: level * LOG_TWO * (1.0 - slope_ref[h])

    def operands(level, p):
        cs = slice(p * LANES, (p + 1) * LANES)
        if level == 0:
            return q_ref[:, cs] * jnp.asarray(0.125, BF), k_ref[:, cs], v_ref[:, cs]
        q = q_lv[level][:, cs]
        if tokens >> level >= 16:
            return q, sib[level][0, :, cs], sib[level][1, :, cs]
        n = sib[level].shape[0] // 16
        both = sib[level][:, cs].astype(F32).reshape(n, 2, 8, LANES)
        k = both[:, 0].reshape(n * 8, LANES).astype(BF)
        return q, k, both[:, 1].reshape(n * 8, LANES).astype(BF)

    def run_units(units):
        qkv = [operands(level, p) for level, p in units]
        scores = [head_scores(q, k) for q, k, _ in qkv]
        weights = [
            head_weights(
                s, (gain_of(level, 2 * p), gain_of(level, 2 * p + 1)), level > 0, tokens >> level
            )
            for s, (level, p) in zip(scores, units)
        ]
        sums = [head_sums(top, pw, v) for (top, pw), (_, _, v) in zip(weights, qkv)]
        for (level, p), parts in zip(units, sums):
            cs = slice(p * LANES, (p + 1) * LANES)
            for i in range(3):
                state[level][i, :, cs] = parts[i]

    def run_levels(*levels):
        run_units([(level, p) for level in levels for p in range(pairs)])

    def forward(level):
        half = half_of(level, core)
        wait_bytes(half, recv_sem.at[level])
        remote(half, half, fsend_sem.at[level], frecv_sem.at[level], other_core).start()

    def w_third(which):
        part = wbuf.at[:, which, :, cols]
        copy = remote(part, part, core_send.at[which], core_recv.at[which], other_core)
        copy.start()

    for p in range(0, pairs, 2):
        run_units([(0, i) for i in range(p, min(p + 2, pairs))])
    forward(2)
    first.wait_recv()
    run_levels(1)
    loop(zs - 1, w_pass)
    w_third(y)
    for level in range(3, last + 1):
        forward(level)
    for level in range(2, last + 1):
        wait_bytes(half_of(level, 1 - core), frecv_sem.at[level])
    run_levels(*range(2, last + 1))
    loop(zs, lambda k: wait_bytes(wbuf.at[(z - k + zs) % zs, 1 - y, :, cols], y_recv.at[k]))
    w_third(1 - y)

    def widen(e, m, den, num):
        e2 = jnp.concatenate([e, e], axis=1)

        def split(x):
            hi = x.astype(BF)
            lo = (x - hi.astype(F32)).astype(BF)
            return dot(e2, jnp.concatenate([hi, lo], axis=0))

        return dot(e, m.astype(BF)), split(den), split(num)

    def merge(a, b):
        top = jnp.maximum(a[0], b[0])
        sa, sb = jnp.exp(a[0] - top), jnp.exp(b[0] - top)
        return top, a[1] * sa + b[1] * sb, a[2] * sa + b[2] * sb

    now = tuple(state[last][i] for i in range(3))
    for level in range(last - 1, 0, -1):
        e = repeat_matrix(rows_at(tokens, level), rows_at(tokens, level + 1))
        now = merge(widen(e, *now), tuple(state[level][i] for i in range(3)))
    e = repeat_matrix(tokens, rows_at(tokens, 1))
    for p in range(pairs):
        cs = slice(p * LANES, (p + 1) * LANES)
        full = widen(e, *(x[:, cs] for x in now))
        full = merge(full, tuple(state[0][i, :, cs] for i in range(3)))
        att[:, cs] = (full[2] / full[1]).astype(BF)

    other_cols = pl.ds(pl.multiple_of((1 - core) * half_w, LANES), half_w)
    for i in range(2):
        wait_bytes(wbuf.at[:, i, :, other_cols], core_recv.at[i])
    if wbuf.shape[2] % 16 == 0:
        w_all = wbuf[...].reshape(width, width)
    else:
        w_all = wbuf[...].astype(F32).reshape(width, width).astype(BF)
    out_ref[...] = dot(att[...], w_all).astype(BF)

    first.wait_send()
    for level in range(2, last + 1):
        half = half_of(level, core)
        wait_bytes(half, send_sem.at[level])
        wait_bytes(half, fsend_sem.at[level])
    part = wbuf.at[z, y, :, cols]
    loop(zs - 1, lambda k: wait_bytes(part, z_send.at[k]))
    loop(zs, lambda k: wait_bytes(part, y_send.at[k]))
    for i in range(2):
        wait_bytes(wbuf.at[:, i, :, cols], core_send.at[i])


def on_device(fine_n, coarse_n, query_rows, key_rows, value_rows, distance_slope, out_weight):
    tokens, width = query_rows.shape
    heads = distance_slope.shape[0]
    last = (fine_n * coarse_n).bit_length() - 1
    levels = range(1, last + 1)
    q_lv = [pltpu.VMEM((rows_at(tokens, l), width), BF) for l in levels]
    own, sib = [], []
    for l in levels:
        if tokens >> l >= 16:
            own.append(pltpu.VMEM((2, tokens >> l, width), BF))
            sib.append(pltpu.VMEM((2, BLOCK, width), BF))
        else:
            own.append(pltpu.VMEM((16, width), BF))
            sib.append(pltpu.VMEM((16 * 2 ** (l - 1), width), BF))
    state = [pltpu.VMEM((3, rows_at(tokens, l), width), F32) for l in range(last + 1)]
    dma = pltpu.SemaphoreType.DMA
    zs = coarse_n // 2
    vmem = pl.BlockSpec(memory_space=pltpu.VMEM)
    return pl.pallas_call(
        functools.partial(kernel, fine_n, coarse_n, tokens, width, heads),
        out_shape=jax.ShapeDtypeStruct((tokens, width), BF),
        in_specs=[pl.BlockSpec(memory_space=pltpu.HBM)] * 5,
        out_specs=vmem,
        scratch_shapes=[pltpu.VMEM((tokens, width), BF)] * 3 + [pltpu.SMEM((heads,), F32)] + q_lv + own + sib + state + [
            pltpu.VMEM((coarse_n // 2, 2) + out_weight.shape, BF),
            pltpu.VMEM((tokens, width), BF),
            dma((last + 1,)), dma((last + 1,)), dma((last + 1,)), dma((last + 1,)),
            dma((5,)), dma((zs,)), dma((zs,)), dma((zs,)), dma((zs,)), dma((2,)), dma((2,)),
        ],
        compiler_params=pltpu.CompilerParams(
            collective_id=0, has_side_effects=True, vmem_limit_bytes=62 * 2**20
        ),
        name="hierarchical_attention",
    )(query_rows, key_rows, value_rows, distance_slope, out_weight)


def solution(mesh):
    fine_n, coarse_n = mesh.shape["fine"], mesh.shape["coarse"]
    return jax.shard_map(
        functools.partial(on_device, fine_n, coarse_n),
        mesh=mesh,
        in_specs=(
            P(("coarse", "fine"), None),
            P(("coarse", "fine"), None),
            P(("coarse", "fine"), None),
            P(),
            P("coarse", None),
        ),
        out_specs=P(("coarse", "fine"), None),
        check_vma=False,
    )
```

```python
import functools
import math

import jax
import jax.numpy as jnp
from jax import lax
from jax.experimental import pallas as pl
from jax.experimental.pallas import tpu as pltpu
from jax.sharding import PartitionSpec as P

BLOCK = 128
LANES = 128
LOG_TWO = math.log(2.0)
NEG = -1e30
BF = jnp.bfloat16
F32 = jnp.float32
MESH = pl.DeviceIdType.MESH


def rows_at(tokens, level):
    return max(16, tokens >> level)


def dot(a, b):
    return jnp.dot(a, b, preferred_element_type=F32)


def grid_ids(rows, cols):
    return (
        lax.broadcasted_iota(jnp.int32, (rows, cols), 0),
        lax.broadcasted_iota(jnp.int32, (rows, cols), 1),
    )


def pair_mean(rows, cols):
    r, c = grid_ids(rows, cols)
    return jnp.where(c // 2 == r, 0.5, 0.0).astype(BF)


def repeat_matrix(rows, cols):
    r, c = grid_ids(rows, cols)
    return jnp.where(r // 2 == c, 1.0, 0.0).astype(BF)


def stacked_mean(which):
    r, c = grid_ids(16, 16)
    if which == "key":
        hit = (r < 8) & (c // 2 == r)
    elif which == "value":
        hit = (r >= 8) & (c // 2 == r - 8)
    else:
        hit = ((r < 8) & (c < 8) & (c // 2 == r)) | (
            (r >= 8) & (c >= 8) & ((c - 8) // 2 == r - 8)
        )
    return jnp.where(hit, 0.5, 0.0).astype(BF)


def loop(count, body):
    if count <= 8:
        for k in range(count):
            body(k)
    else:

        def step(k, carry):
            body(k)
            return carry

        lax.fori_loop(0, count, step, 0)


def wait_bytes(ref, sem):
    pltpu.make_async_copy(ref, ref, sem).wait()


def head_scores(q, k):
    left = lax.broadcasted_iota(jnp.int32, (1, LANES), 1) < LANES // 2
    zero = jnp.zeros_like(q)
    q2 = jnp.concatenate([jnp.where(left, q, zero), jnp.where(left, zero, q)], axis=0)
    return lax.dot_general(q2, k, (((1,), (1,)), ((), ())), preferred_element_type=F32)


def head_weights(s, gains, coarse_ref, valid):
    if valid < 8:
        key_no = lax.broadcasted_iota(jnp.int32, (1, s.shape[1]), 1)
        s = jnp.where(key_no % 8 < valid, s, NEG)
    top = jnp.max(s, axis=1, keepdims=True)
    if not coarse_ref:
        return top, jnp.exp(s - top).astype(BF)
    rows = s.shape[0] // 2
    row_no = lax.broadcasted_iota(jnp.int32, (2 * rows, 1), 0)
    gain = jnp.where(row_no < rows, gains[0], gains[1])
    top = (top + gain).astype(BF).astype(F32)
    return top, jnp.exp(s - (top - gain)).astype(BF)


def head_sums(top, p, v):
    rows = p.shape[0] // 2
    left = lax.broadcasted_iota(jnp.int32, (1, LANES), 1) < LANES // 2
    o = dot(p, jnp.concatenate([v, jnp.ones(v.shape, BF)], axis=1))
    top = jnp.broadcast_to(top, (2 * rows, LANES))
    pick = lambda x: jnp.where(left, x[:rows], x[rows:])
    return pick(top), pick(o[:, LANES:]), pick(o[:, :LANES])


def kernel(fine_n, coarse_n, tokens, width, heads, *refs):
    n_dev = fine_n * coarse_n
    fine_bits = fine_n.bit_length() - 2
    last = n_dev.bit_length() - 1
    pairs = width // LANES
    half_w = width // 2
    zs = coarse_n // 2
    it = iter(refs)
    q_hbm, k_hbm, v_hbm, slope_hbm, w_ref, out_ref = (next(it) for _ in range(6))
    q_ref, k_ref, v_ref, slope_ref = (next(it) for _ in range(4))
    q_lv = [None] + [next(it) for _ in range(last)]
    own = [None] + [next(it) for _ in range(last)]
    sib = [None] + [next(it) for _ in range(last)]
    state = [next(it) for _ in range(last + 1)]
    wbuf = next(it)
    att = next(it)
    send_sem, recv_sem, fsend_sem, frecv_sem = (next(it) for _ in range(4))
    load_sem, z_send, z_recv, y_send, y_recv, core_send, core_recv = (next(it) for _ in range(7))

    f = lax.axis_index("fine")
    c = lax.axis_index("coarse")
    dev = c * fine_n + f
    core = f % 2
    chip = dev // 2
    z = c // 2
    y = c % 2
    cols = pl.ds(pl.multiple_of(core * half_w, LANES), half_w)

    def at(chip_no):
        d = chip_no * 2 + core
        return {"fine": d % fine_n, "coarse": d // fine_n}

    def flip(bit):
        return chip + (1 - 2 * (chip // 2**bit % 2)) * 2**bit

    other_core = {"fine": f + 1 - 2 * core, "coarse": c}
    flip_y = {"fine": f, "coarse": c + 1 - 2 * y}

    loads = [
        pltpu.make_async_copy(a, b, load_sem.at[i])
        for i, (a, b) in enumerate(
            (
                (k_hbm, k_ref),
                (v_hbm, v_ref),
                (q_hbm, q_ref),
                (w_ref.at[:, cols], wbuf.at[z, y, :, cols]),
                (slope_hbm, slope_ref),
            )
        )
    ]
    for load in loads:
        load.start()

    barrier = pltpu.get_barrier_semaphore()
    pl.semaphore_signal(barrier, inc=1, device_id=other_core, device_id_type=MESH)

    pl.semaphore_signal(barrier, inc=1, device_id=flip_y, device_id_type=MESH)
    for bit in range(fine_bits):
        pl.semaphore_signal(barrier, inc=1, device_id=at(flip(bit)), device_id_type=MESH)

    def greet(k):
        peer = {"fine": f, "coarse": (z + k + 1) % zs * 2 + y}
        pl.semaphore_signal(barrier, inc=1, device_id=peer, device_id_type=MESH)

    loop(zs - 1, greet)

    for load in loads:
        load.wait()

    for level in range(1, last + 1):
        rows, prev = rows_at(tokens, level), rows_at(tokens, level - 1)
        mean = pair_mean(rows, prev)
        if level == 1:
            q_prev, k_prev, v_prev = q_ref[...] * jnp.asarray(0.125, BF), k_ref[...], v_ref[...]
        q_prev = dot(mean, q_prev).astype(BF)
        q_lv[level][...] = q_prev
        if tokens >> level >= 16:
            k_prev = dot(mean, k_prev).astype(BF)
            v_prev = dot(mean, v_prev).astype(BF)
            own[level][0] = k_prev
            own[level][1] = v_prev
        else:
            if tokens >> level == 8:
                both = dot(stacked_mean("key"), k_prev) + dot(stacked_mean("value"), v_prev)
            else:
                both = dot(stacked_mean("both"), both)
            both = both.astype(BF)
            own[level][...] = both

    pl.semaphore_wait(barrier, 1 + fine_bits + zs)

    def remote(src, dst, s_sem, r_sem, dev_id):
        return pltpu.make_async_remote_copy(
            src_ref=src, dst_ref=dst, send_sem=s_sem, recv_sem=r_sem,
            device_id=dev_id, device_id_type=MESH,
        )

    def w_first(k):
        z_to = (z + k + 1) % zs
        remote(
            wbuf.at[z, y, :, cols], wbuf.at[z, y, :, cols], z_send.at[k], z_recv.at[k],
            {"fine": f, "coarse": z_to * 2 + y},
        ).start()

    def w_second(k, z_from):
        part = wbuf.at[z_from, y, :, cols]
        remote(part, part, y_send.at[k], y_recv.at[k], flip_y).start()

    def w_pass(k):
        z_from = (z - (k + 1) + zs) % zs
        wait_bytes(wbuf.at[z_from, y, :, cols], z_recv.at[k])
        w_second(k + 1, z_from)

    def half_of(level, which):
        if tokens >> level >= 16:
            return sib[level].at[:, pl.ds(pl.multiple_of(which * 64, 16), 64), :]
        n = sib[level].shape[0] // 2
        return sib[level].at[pl.ds(pl.multiple_of(which * n, 16), n), :]

    def block_of(level, start, count):
        group = 2 ** (level - 2)
        if tokens >> level >= 16:
            rows = tokens >> level
            at_row = pl.multiple_of(core * 64 + start * rows, 16)
            return sib[level].at[:, pl.ds(at_row, rows * count), :]
        return sib[level].at[pl.ds(pl.multiple_of((core * group + start) * 16, 16), 16 * count), :]

    def piece(level, step):
        group = 2 ** (level - 2)
        mine = chip % group
        if step == 0:
            here = block_of(level, mine, 1)
            return own[level], here, level - 2, here
        width_b = 2 ** (step - 1)
        n = mine // width_b
        here = block_of(level, n * width_b, width_b)
        there = block_of(level, (n + 1 - 2 * (n % 2)) * width_b, width_b)
        return here, here, step - 1, there

    def exchange(step):
        for level in range(max(2, step + 1), last + 1):
            if step >= 1:
                got = piece(level, step - 1)[3]
                wait_bytes(got, recv_sem.at[level * last + step - 1])
            if step <= level - 2:
                src, dst, bit, _ = piece(level, step)
                sem = level * last + step
                remote(src, dst, send_sem.at[sem], recv_sem.at[sem], at(flip(bit))).start()
            else:
                half = half_of(level, core)
                remote(half, half, fsend_sem.at[level], frecv_sem.at[level], other_core).start()

    first = remote(own[1], sib[1], send_sem.at[1], recv_sem.at[1], other_core)
    first.start()
    exchange(0)
    w_second(0, z)
    loop(zs - 1, w_first)

    gain_of = lambda level, h: level * LOG_TWO * (1.0 - slope_ref[h])

    def operands(level, p):
        cs = slice(p * LANES, (p + 1) * LANES)
        if level == 0:
            return q_ref[:, cs] * jnp.asarray(0.125, BF), k_ref[:, cs], v_ref[:, cs]
        q = q_lv[level][:, cs]
        if tokens >> level >= 16:
            return q, sib[level][0, :, cs], sib[level][1, :, cs]
        n = sib[level].shape[0] // 16
        both = sib[level][:, cs].astype(F32).reshape(n, 2, 8, LANES)
        k = both[:, 0].reshape(n * 8, LANES).astype(BF)
        return q, k, both[:, 1].reshape(n * 8, LANES).astype(BF)

    def run_units(units):
        qkv = [operands(level, p) for level, p in units]
        scores = [head_scores(q, k) for q, k, _ in qkv]
        weights = [
            head_weights(
                s, (gain_of(level, 2 * p), gain_of(level, 2 * p + 1)), level > 0, tokens >> level
            )
            for s, (level, p) in zip(scores, units)
        ]
        sums = [head_sums(top, pw, v) for (top, pw), (_, _, v) in zip(weights, qkv)]
        for (level, p), parts in zip(units, sums):
            cs = slice(p * LANES, (p + 1) * LANES)
            for i in range(3):
                state[level][i, :, cs] = parts[i]

    def run_levels(*levels):
        run_units([(level, p) for level in levels for p in range(pairs)])

    def w_third(which):
        part = wbuf.at[:, which, :, cols]
        copy = remote(part, part, core_send.at[which], core_recv.at[which], other_core)
        copy.start()

    for p in range(0, pairs, 2):
        run_units([(0, i) for i in range(p, min(p + 2, pairs))])
        if p // 2 + 1 < last:
            exchange(p // 2 + 1)
    first.wait_recv()
    for step in range((pairs + 1) // 2 + 1, last):
        exchange(step)
    run_levels(1)
    loop(zs - 1, w_pass)
    w_third(y)
    for level in range(2, last + 1):
        wait_bytes(half_of(level, 1 - core), frecv_sem.at[level])
    run_levels(*range(2, last + 1))
    loop(zs, lambda k: wait_bytes(wbuf.at[(z - k + zs) % zs, 1 - y, :, cols], y_recv.at[k]))
    w_third(1 - y)

    def widen(e, m, den, num):
        e2 = jnp.concatenate([e, e], axis=1)

        def split(x):
            hi = x.astype(BF)
            lo = (x - hi.astype(F32)).astype(BF)
            return dot(e2, jnp.concatenate([hi, lo], axis=0))

        return dot(e, m.astype(BF)), split(den), split(num)

    def merge(a, b):
        top = jnp.maximum(a[0], b[0])
        sa, sb = jnp.exp(a[0] - top), jnp.exp(b[0] - top)
        return top, a[1] * sa + b[1] * sb, a[2] * sa + b[2] * sb

    now = tuple(state[last][i] for i in range(3))
    for level in range(last - 1, 0, -1):
        e = repeat_matrix(rows_at(tokens, level), rows_at(tokens, level + 1))
        now = merge(widen(e, *now), tuple(state[level][i] for i in range(3)))
    e = repeat_matrix(tokens, rows_at(tokens, 1))
    for p in range(pairs):
        cs = slice(p * LANES, (p + 1) * LANES)
        full = widen(e, *(x[:, cs] for x in now))
        full = merge(full, tuple(state[0][i, :, cs] for i in range(3)))
        att[:, cs] = (full[2] / full[1]).astype(BF)

    other_cols = pl.ds(pl.multiple_of((1 - core) * half_w, LANES), half_w)
    for i in range(2):
        wait_bytes(wbuf.at[:, i, :, other_cols], core_recv.at[i])
    if wbuf.shape[2] % 16 == 0:
        w_all = wbuf[...].reshape(width, width)
    else:
        w_all = wbuf[...].astype(F32).reshape(width, width).astype(BF)
    out_ref[...] = dot(att[...], w_all).astype(BF)

    first.wait_send()
    for level in range(2, last + 1):
        half = half_of(level, core)
        for step in range(level - 1):
            wait_bytes(piece(level, step)[0], send_sem.at[level * last + step])
        wait_bytes(half, fsend_sem.at[level])
    part = wbuf.at[z, y, :, cols]
    loop(zs - 1, lambda k: wait_bytes(part, z_send.at[k]))
    loop(zs, lambda k: wait_bytes(part, y_send.at[k]))
    for i in range(2):
        wait_bytes(wbuf.at[:, i, :, cols], core_send.at[i])


def on_device(fine_n, coarse_n, query_rows, key_rows, value_rows, distance_slope, out_weight):
    tokens, width = query_rows.shape
    heads = distance_slope.shape[0]
    last = (fine_n * coarse_n).bit_length() - 1
    levels = range(1, last + 1)
    q_lv = [pltpu.VMEM((rows_at(tokens, l), width), BF) for l in levels]
    own, sib = [], []
    for l in levels:
        if tokens >> l >= 16:
            own.append(pltpu.VMEM((2, tokens >> l, width), BF))
            sib.append(pltpu.VMEM((2, BLOCK, width), BF))
        else:
            own.append(pltpu.VMEM((16, width), BF))
            sib.append(pltpu.VMEM((16 * 2 ** (l - 1), width), BF))
    state = [pltpu.VMEM((3, rows_at(tokens, l), width), F32) for l in range(last + 1)]
    dma = pltpu.SemaphoreType.DMA
    zs = coarse_n // 2
    vmem = pl.BlockSpec(memory_space=pltpu.VMEM)
    return pl.pallas_call(
        functools.partial(kernel, fine_n, coarse_n, tokens, width, heads),
        out_shape=jax.ShapeDtypeStruct((tokens, width), BF),
        in_specs=[pl.BlockSpec(memory_space=pltpu.HBM)] * 5,
        out_specs=vmem,
        scratch_shapes=[pltpu.VMEM((tokens, width), BF)] * 3 + [pltpu.SMEM((heads,), F32)] + q_lv + own + sib + state + [
            pltpu.VMEM((coarse_n // 2, 2) + out_weight.shape, BF),
            pltpu.VMEM((tokens, width), BF),
            dma(((last + 1) * last,)), dma(((last + 1) * last,)), dma((last + 1,)), dma((last + 1,)),
            dma((5,)), dma((zs,)), dma((zs,)), dma((zs,)), dma((zs,)), dma((2,)), dma((2,)),
        ],
        compiler_params=pltpu.CompilerParams(
            collective_id=0, has_side_effects=True, vmem_limit_bytes=62 * 2**20
        ),
        name="hierarchical_attention",
    )(query_rows, key_rows, value_rows, distance_slope, out_weight)


def solution(mesh):
    fine_n, coarse_n = mesh.shape["fine"], mesh.shape["coarse"]
    return jax.shard_map(
        functools.partial(on_device, fine_n, coarse_n),
        mesh=mesh,
        in_specs=(
            P(("coarse", "fine"), None),
            P(("coarse", "fine"), None),
            P(("coarse", "fine"), None),
            P(),
            P("coarse", None),
        ),
        out_specs=P(("coarse", "fine"), None),
        check_vma=False,
    )
```
